32 devices in a mesh: row: 4 (over z), col: 8 (over y, x, core).
Axes of the slice: x: 2, y: 2, z: 4, core: 2. Of those that a mesh axis runs over, the one named last changes fastest.
Arguments:
- rhs_super: bfloat16 [2, 4, 4, 128, 512], P(None, None, 'row'), may hold values from -6 to 6
- factor_super: bfloat16 [2, 4, 4, 128, 4, 8, 128], P(None, None, 'row', None, None, 'col'), may hold values from -0.125 to 0.125
- mask_super: int32 [2, 4, 4, 4, 8], P(None, None, 'row', None, 'col'), may hold values 0 or 1
- dinv_rows: bfloat16 [4, 8, 128, 2048], P(None, 'col'), may hold values from -0.125 to 0.125
- factor_trail: bfloat16 [8, 4, 128, 4, 8, 128], P(None, 'row', None, None, 'col'), may hold values from -0.125 to 0.125
- mask_trail: int32 [8, 4, 4, 8], P(None, 'row', None, 'col'), may hold values 0 or 1
- rhs_trail: bfloat16 [8, 1, 4, 128, 512], P('col', None, 'row'), may hold values from -6 to 6
Outputs:
- solved: bfloat16 [4, 8, 128, 512], P(None, 'col')
- remaining: bfloat16 [8, 1, 4, 128, 512], P('col', None, 'row')
The draws below stay inside these ranges and needn't reach their ends.
All inputs are finite; a program needn't handle non-finite values. No bound on the sum of `mask_super` or of `mask_trail` on one device may be relied on, other than what follows from the above.
Results may differ from the reference program's by a relative error of at most 0.0048.
Values may be sent and summed in bfloat16 or wider, within the bound.
A program may use at most 64 MiB of HBM per device.

```python
import jax
import jax.numpy as jnp

TB = 128
ST = 16
NSB = 2
K = 512
TQ = 1
SB = 2048
NS = 4096
SQ = 4
JT_DEV = 4
ITR = 8
N_ROW = 4
N_COL = 8


def touch_ends(entries, stream_key, least, high):
    longest = entries.shape.index(max(entries.shape))
    spots = []
    for shift in (0, 1):
        where = [jax.random.randint(jax.random.fold_in(stream_key, axis), (), 0, length) for axis, length in enumerate(entries.shape)]
        where[longest] = (where[longest] + shift) % entries.shape[longest]
        spots.append(tuple(where))
    return entries.at[spots[0]].set(least).at[spots[1]].set(high)


def levels(stream_key, extent, split, smallest, largest):
    loudness, own = 1.0, jax.random.fold_in(stream_key, 6)
    for axis_at, shards_of in split:
        draws = jnp.exp(jax.random.uniform(jax.random.fold_in(own, axis_at), (shards_of,), jnp.float32, smallest / len(split), largest / len(split)))
        loudness = loudness * jnp.repeat(draws, extent[axis_at] // shards_of).reshape([-1 if axis == axis_at else 1 for axis in range(len(extent))])
    return loudness


def gaussian(own_key, extent, spread, bound, split=(), held_as=jnp.bfloat16):
    gain = levels(own_key, extent, split, -0.22, 0.18) if split else 1.0
    values = jax.random.normal(own_key, extent, jnp.float32) * spread * gain
    return jnp.minimum(jnp.maximum(values, -bound), bound).astype(held_as)


def setup_inputs(seed: int = 0) -> dict:
    keys = jax.random.split(jax.random.key(seed), 8)
    return {
        "rhs_super": gaussian(keys[0], (NSB, SQ, N_ROW, TB, K), 1.0, 6.0, ((2, 4),)),
        "factor_super": gaussian(keys[1], (NSB, SQ, N_ROW, TB, JT_DEV, N_COL, TB), SB ** -0.5, 0.125, ((2, 4), (5, 8))),
        "mask_super": touch_ends((jax.random.randint(keys[2], (NSB, SQ, N_ROW, JT_DEV, N_COL), 0, 2) < 1).astype(jnp.int32), jax.random.fold_in(keys[2], 1), 0, 1),
        "dinv_rows": gaussian(keys[3], (JT_DEV, N_COL, TB, SB), SB ** -0.5, 0.125, ((1, 8),)),
        "factor_trail": gaussian(keys[4], (ITR, N_ROW, TB, JT_DEV, N_COL, TB), (NS // 2) ** -0.5, 0.125, ((1, 4), (4, 8))),
        "mask_trail": touch_ends((jax.random.randint(keys[5], (ITR, N_ROW, JT_DEV, N_COL), 0, 2) < 1).astype(jnp.int32), jax.random.fold_in(keys[5], 1), 0, 1),
        "rhs_trail": gaussian(keys[6], (N_COL, TQ, N_ROW, TB, K), 1.0, 6.0, ((0, 8), (2, 4))),
    }


def reference(rhs_super, factor_super, mask_super, dinv_rows, factor_trail, mask_trail, rhs_trail):
    tile_count = NSB * ST
    solved_count = tile_count * TB
    block_rows = ST * TB
    owners = jnp.arange(tile_count, dtype=jnp.int32) // ST
    earlier = (owners[:, None] > owners[None, :]).astype(jnp.int32)
    keep_super = (mask_super.reshape(tile_count, tile_count) * earlier).astype(jnp.bfloat16)
    lower_tiles = factor_super.reshape(tile_count, TB, tile_count, TB) * keep_super[:, None, :, None]
    lower_tiles = lower_tiles.reshape(solved_count, solved_count)
    inverse = dinv_rows.reshape(NSB, block_rows, block_rows)
    given_rows = rhs_super.reshape(NSB, block_rows, K)
    solved = jnp.zeros((solved_count, K), jnp.bfloat16)
    for block in range(NSB):
        reached = jnp.dot(lower_tiles[block * block_rows:(block + 1) * block_rows], solved, preferred_element_type=jnp.float32)
        due_rows = (given_rows[block].astype(jnp.float32) - reached).astype(jnp.bfloat16)
        freshly = jnp.dot(inverse[block], due_rows, preferred_element_type=jnp.float32).astype(jnp.bfloat16)
        solved = solved.at[block * block_rows:(block + 1) * block_rows].set(freshly)
    keep_trail = mask_trail.astype(jnp.bfloat16)[:, :, None, :, :, None]
    trail_tiles = (factor_trail * keep_trail).reshape(-1, solved_count)
    reached = jnp.dot(trail_tiles, solved, preferred_element_type=jnp.float32)
    remaining = (rhs_trail.reshape(-1, K).astype(jnp.float32) - reached).astype(jnp.bfloat16)
    return solved.reshape(dinv_rows.shape[0], dinv_rows.shape[1], TB, K), remaining.reshape(rhs_trail.shape)
```

```python
import functools

import jax
import jax.numpy as jnp
from jax import lax
from jax.experimental import pallas as pl
from jax.experimental.pallas import tpu as pltpu
from jax.sharding import PartitionSpec as P

TB = 128
ST = 16
NSB = 2


def plain_body(rhs_super, factor_super, mask_super, dinv_rows, factor_trail, mask_trail, rhs_trail):
    width_k = rhs_super.shape[-1]
    per_col = dinv_rows.shape[0]
    per_row = rhs_super.shape[1]
    block_rows = dinv_rows.shape[-1]
    column_here = lax.axis_index("col")
    owners = (jnp.arange(per_col, dtype=jnp.int32) * lax.axis_size("col") + column_here) // ST
    solved = jnp.zeros((per_col, 1, TB, width_k), jnp.bfloat16)
    for block in range(NSB):
        due_rows = rhs_super[block]
        if block > 0:
            allowed = (owners < block).astype(jnp.int32)
            keep_tiles = (mask_super[block] * allowed[None, None, :, None]).astype(jnp.bfloat16)
            masked = factor_super[block] * keep_tiles[:, :, None, :, :, None]
            partial_sum = jnp.dot(
                masked.reshape(per_row * TB, per_col * TB),
                solved.reshape(per_col * TB, width_k),
                preferred_element_type=jnp.float32,
            )
            reached = lax.psum(partial_sum, "col")
            due_rows = (
                (due_rows.reshape(per_row * TB, width_k).astype(jnp.float32) - reached)
                .astype(jnp.bfloat16)
                .reshape(due_rows.shape)
            )
        gathered = lax.all_gather(due_rows, "row", axis=1, tiled=True).reshape(block_rows, width_k)
        columns = []
        for position in range(per_col):

            def compute(position=position):
                return jnp.dot(
                    dinv_rows[position, 0], gathered, preferred_element_type=jnp.float32
                ).astype(jnp.bfloat16)

            def retain(position=position):
                return solved[position, 0]

            columns.append(lax.cond(owners[position] == block, compute, retain))
        solved = jnp.stack(columns)[:, None]
    keep_trail = mask_trail.astype(jnp.bfloat16)[:, :, None, :, :, None]
    masked_trail = factor_trail * keep_trail
    share = rhs_trail.shape[1]
    moved = lax.all_to_all(masked_trail, "col", split_axis=0, concat_axis=4, tiled=True)
    reached = jnp.dot(
        moved.reshape(share * TB, -1),
        lax.all_gather(solved, "col", axis=1, tiled=True).reshape(-1, width_k),
        preferred_element_type=jnp.float32,
    )
    remaining = (rhs_trail.reshape(share * TB, width_k).astype(jnp.float32) - reached).astype(
        jnp.bfloat16
    )
    return (solved, remaining.reshape(rhs_trail.shape))


MESH = pl.DeviceIdType.MESH
F32 = jnp.float32
BF16 = jnp.bfloat16


def kernel(
    n_row, n_col,
    rhs_s, fac_s, mask_s, dinv, fac_t, mask_t, rhs_t,
    solved_o, rem_o,
    dinv_v, facs_v, fact_v, rhst_v, ltri, due0, due1, share1, part, rs0, solv, lt, acc, tpart, trs,
    local_sem, z_send, z_recv, l_send, l_recv, g_send, g_recv, p_send, p_recv, s_send, s_recv, t_send, t_recv,
):
    per_sb = dinv_v.shape[0] // NSB
    per_col = dinv_v.shape[0]
    sq_count, halves, sh, kr = due0.shape[0], due0.shape[2], due0.shape[3], due0.shape[4]
    tiles_t = lt.shape[0] // TB
    cols = per_sb * TB
    r, c = lax.axis_index("row"), lax.axis_index("col")
    sq, half = c // halves, c % halves
    rows_at = lambda d: lax.rem(r + d, n_row)
    cols_at = lambda d: lax.rem(c + d, n_col)

    barrier = pltpu.get_barrier_semaphore()
    for d in range(1, n_row):
        pl.semaphore_signal(barrier, inc=1, device_id=(rows_at(d), c), device_id_type=MESH)
    for d in range(1, n_col):
        pl.semaphore_signal(barrier, inc=1, device_id=(r, cols_at(d)), device_id_type=MESH)

    def kslice(k):
        return pl.ds(pl.multiple_of(k * kr, kr), kr)

    own_rows = pl.ds(pl.multiple_of(half * sh, sh), sh)
    local = [
        pltpu.make_async_copy(fac_s.at[1], facs_v, local_sem.at[0]),
        pltpu.make_async_copy(rhs_s.at[0, sq, own_rows, kslice(r)], due0.at[sq, r, half], local_sem.at[1]),
        pltpu.make_async_copy(rhs_s.at[1, sq, own_rows, kslice(r)], share1.at[r], local_sem.at[2]),
        pltpu.make_async_copy(dinv, dinv_v, local_sem.at[3]),
        pltpu.make_async_copy(fac_t, fact_v, local_sem.at[4]),
        pltpu.make_async_copy(rhs_t, rhst_v, local_sem.at[5]),
    ]
    for copy in local:
        copy.start()
    pl.semaphore_wait(barrier, n_row - 1 + n_col - 1)

    def remote(src, dst, send, recv, device):
        copy = pltpu.make_async_remote_copy(
            src_ref=src, dst_ref=dst, send_sem=send, recv_sem=recv, device_id=device, device_id_type=MESH
        )
        copy.start()
        return copy

    z_copies = []
    for s in range(NSB):
        for d in range(1, n_row):
            to = rows_at(d)
            dst = due0.at[sq, r, half] if s == 0 else share1.at[r]
            z_copies.append(remote(
                rhs_s.at[s, sq, own_rows, kslice(to)], dst, z_send.at[s, d - 1], z_recv.at[s, d - 1], (to, c)))

    def sorter(count):
        shape = (count * TB, per_col * TB)
        a = lax.broadcasted_iota(jnp.int32, shape, 0)
        b = lax.broadcasted_iota(jnp.int32, shape, 1)
        return (b == (a % TB) * per_col + a // TB).astype(F32).astype(BF16)

    local[0].wait()
    sort_few = sorter(per_sb)
    for q in range(sq_count):
        tiles = jnp.dot(sort_few, facs_v[q], preferred_element_type=F32)
        for p in range(per_sb):
            kept = tiles[p * TB:(p + 1) * TB] * mask_s[1, q, p].astype(F32)
            ltri[r, q, :, p * TB:(p + 1) * TB] = kept.astype(BF16)
    l_copies = [
        remote(ltri.at[r], ltri.at[r], l_send.at[d - 1], l_recv.at[d - 1], (rows_at(d), c)) for d in range(1, n_row)
    ]

    def gather(due, s):
        return [
            remote(due.at[sq, :, half], due.at[sq, :, half], g_send.at[s, d - 1], g_recv.at[s, d - 1], (r, cols_at(d)))
            for d in range(1, n_col)
        ]

    def spread(s):
        return [
            remote(solv.at[s, r], solv.at[s, r], s_send.at[s, d - 1], s_recv.at[s, d - 1], (rows_at(d), c))
            for d in range(1, n_row)
        ]

    def solve(due, s):
        block = dinv_v[s * per_sb:(s + 1) * per_sb].reshape(cols, -1)
        fresh = jnp.dot(block, due[...].reshape(-1, kr), preferred_element_type=F32).astype(BF16)
        solv[s, r] = fresh
        return fresh

    local[1].wait()
    for copy in z_copies[:n_row - 1]:
        copy.wait_recv()
    g0 = gather(due0, 0)
    local[3].wait()
    for copy in g0:
        copy.wait_recv()
    fresh = solve(due0, 0)
    s0 = spread(0)

    for d in range(n_row):
        at = rows_at(n_row - d)
        if d > 0:
            l_copies[d - 1].wait_recv()
        update = jnp.dot(ltri[at].reshape(-1, cols), fresh, preferred_element_type=F32).astype(BF16)
        part[:, at] = update.reshape(sq_count, halves, sh, kr)
    p_copies = []
    for d in range(1, n_col):
        to = cols_at(d)
        p_copies.append(remote(
            part.at[to // halves, :, to % halves], rs0.at[d - 1], p_send.at[d - 1], p_recv.at[d - 1], (r, to)))

    local[4].wait()
    sort_all = sorter(per_col)

    def order(i, _):
        tiles = jnp.dot(sort_all, fact_v[i], preferred_element_type=F32)
        for p in range(per_col):
            kept = tiles[p * TB:(p + 1) * TB] * mask_t[i, p].astype(F32)
            lt[pl.ds(pl.multiple_of(i * TB, TB), TB), p * TB:(p + 1) * TB] = kept.astype(BF16)
        return 0

    lax.fori_loop(0, tiles_t, order, 0)

    local[2].wait()
    for copy in z_copies[n_row - 1:]:
        copy.wait_recv()
    reached = part[sq, :, half].astype(F32)
    for d in range(1, n_col):
        p_copies[d - 1].wait_recv()
        reached += rs0[d - 1].astype(F32)
    due1[sq, :, half] = (share1[...].astype(F32) - reached).astype(BF16)
    g1 = gather(due1, 1)

    for d in range(n_row):
        at = rows_at(n_row - d)
        if d > 0:
            s0[d - 1].wait_recv()
        acc[at] = jnp.dot(lt[:, :cols], solv[0, at], preferred_element_type=F32)

    for copy in g1:
        copy.wait_recv()
    solve(due1, 1)
    s1 = spread(1)

    t_copies = []
    for d in range(n_row):
        at = rows_at(n_row - d)
        if d > 0:
            s1[d - 1].wait_recv()
        update = acc[at] + jnp.dot(lt[:, cols:], solv[1, at], preferred_element_type=F32)
        tpart[at] = update.astype(BF16).reshape(n_col, -1, kr)
        t_copies.append([
            remote(tpart.at[at, cols_at(e)], trs.at[d, e - 1], t_send.at[d, e - 1], t_recv.at[d, e - 1], (r, cols_at(e)))
            for e in range(1, n_col)
        ])
    for s in range(NSB):
        for k in range(n_row):
            solved_o[s * per_sb:(s + 1) * per_sb, :, k * kr:(k + 1) * kr] = solv[s, k].reshape(per_sb, TB, kr)
    local[5].wait()
    for d in range(n_row):
        at = rows_at(n_row - d)
        reached = tpart[at, c].astype(F32)
        for e in range(1, n_col):
            t_copies[d][e - 1].wait_recv()
            reached += trs[d, e - 1].astype(F32)
        rem_o[:, kslice(at)] = (rhst_v[:, kslice(at)].astype(F32) - reached).astype(BF16)

    for copy in z_copies + l_copies + g0 + s0 + p_copies + g1 + s1 + sum(t_copies, []):
        copy.wait_send()


def fast_body(n_row, n_col, rhs_super, factor_super, mask_super, dinv_rows, factor_trail, mask_trail, rhs_trail):
    width_k = rhs_super.shape[-1]
    sq_count = rhs_super.shape[1]
    per_col = dinv_rows.shape[0]
    tiles_t = factor_trail.shape[0]
    share_t = rhs_trail.shape[1]
    per_sb = per_col // NSB
    cols = per_sb * TB
    kr = width_k // n_row
    sh = sq_count * TB // n_col
    halves = TB // sh
    vmem = lambda *shape: pltpu.VMEM(shape, BF16)
    dma = lambda *shape: pltpu.SemaphoreType.DMA(shape)
    due_shape = (sq_count, n_row, halves, sh, kr)
    anywhere = pl.BlockSpec(memory_space=pl.ANY)
    scalars = pl.BlockSpec(memory_space=pltpu.SMEM)
    whole = pl.BlockSpec(memory_space=pltpu.VMEM)
    solved, remaining = pl.pallas_call(
        functools.partial(kernel, n_row, n_col),
        out_shape=(
            jax.ShapeDtypeStruct((per_col, TB, width_k), BF16),
            jax.ShapeDtypeStruct((share_t * TB, width_k), BF16),
        ),
        in_specs=[anywhere, anywhere, scalars, anywhere, anywhere, scalars, anywhere],
        out_specs=(whole, whole),
        scratch_shapes=[
            vmem(per_col, TB, dinv_rows.shape[-1]),
            vmem(sq_count, TB * per_col, TB),
            vmem(tiles_t, TB * per_col, TB),
            vmem(share_t * TB, width_k),
            vmem(n_row, sq_count, TB, cols),
            vmem(*due_shape),
            vmem(*due_shape),
            vmem(n_row, sh, kr),
            vmem(*due_shape),
            vmem(n_col - 1, n_row, sh, kr),
            vmem(NSB, n_row, cols, kr),
            vmem(tiles_t * TB, per_col * TB),
            pltpu.VMEM((n_row, tiles_t * TB, kr), F32),
            vmem(n_row, n_col, share_t * TB, kr),
            vmem(n_row, n_col - 1, share_t * TB, kr),
            dma(6),
            dma(NSB, n_row - 1), dma(NSB, n_row - 1),
            dma(n_row - 1), dma(n_row - 1),
            dma(NSB, n_col - 1), dma(NSB, n_col - 1),
            dma(n_col - 1), dma(n_col - 1),
            dma(NSB, n_row - 1), dma(NSB, n_row - 1),
            dma(n_row, n_col - 1), dma(n_row, n_col - 1),
        ],
        compiler_params=pltpu.CompilerParams(
            collective_id=0, has_side_effects=True, vmem_limit_bytes=40 * 1024 * 1024
        ),
    )(
        rhs_super.reshape(NSB, sq_count, TB, width_k),
        factor_super.reshape(NSB, sq_count, TB * per_col, TB),
        mask_super.reshape(NSB, sq_count, per_col),
        dinv_rows.reshape(per_col, TB, -1),
        factor_trail.reshape(tiles_t, TB * per_col, TB),
        mask_trail.reshape(tiles_t, per_col),
        rhs_trail.reshape(share_t * TB, width_k),
    )
    return solved[:, None], remaining.reshape(rhs_trail.shape)


def body_for(mesh):
    n_row, n_col = mesh.shape["row"], mesh.shape["col"]

    def body(rhs_super, factor_super, mask_super, dinv_rows, factor_trail, mask_trail, rhs_trail):
        args = (rhs_super, factor_super, mask_super, dinv_rows, factor_trail, mask_trail, rhs_trail)
        due_rows = rhs_super.shape[1] * TB
        fits = (
            ST % n_col == 0
            and due_rows % n_col == 0
            and TB % (due_rows // n_col) == 0
            and (due_rows // n_col) % 16 == 0
            and rhs_super.shape[-1] % (n_row * 128) == 0
        )
        return fast_body(n_row, n_col, *args) if fits else plain_body(*args)

    return body


def solution(mesh):
    placed = (
        P(None, None, "row", None, None),
        P(None, None, "row", None, None, "col", None),
        P(None, None, "row", None, "col"),
        P(None, "col", None, None),
        P(None, "row", None, None, "col", None),
        P(None, "row", None, "col"),
        P("col", None, "row", None, None),
    )
    return jax.shard_map(
        body_for(mesh),
        mesh=mesh,
        in_specs=placed,
        out_specs=(P(None, "col", None, None), P("col", None, "row", None, None)),
        check_vma=False,
    )
```

```python
import functools

import jax
import jax.numpy as jnp
from jax import lax
from jax.experimental import pallas as pl
from jax.experimental.pallas import tpu as pltpu
from jax.sharding import PartitionSpec as P

TB = 128
ST = 16
NSB = 2


def plain_body(rhs_super, factor_super, mask_super, dinv_rows, factor_trail, mask_trail, rhs_trail):
    width_k = rhs_super.shape[-1]
    per_col = dinv_rows.shape[0]
    per_row = rhs_super.shape[1]
    block_rows = dinv_rows.shape[-1]
    column_here = lax.axis_index("col")
    owners = (jnp.arange(per_col, dtype=jnp.int32) * lax.axis_size("col") + column_here) // ST
    solved = jnp.zeros((per_col, 1, TB, width_k), jnp.bfloat16)
    for block in range(NSB):
        due_rows = rhs_super[block]
        if block > 0:
            allowed = (owners < block).astype(jnp.int32)
            keep_tiles = (mask_super[block] * allowed[None, None, :, None]).astype(jnp.bfloat16)
            masked = factor_super[block] * keep_tiles[:, :, None, :, :, None]
            partial_sum = jnp.dot(
                masked.reshape(per_row * TB, per_col * TB),
                solved.reshape(per_col * TB, width_k),
                preferred_element_type=jnp.float32,
            )
            reached = lax.psum(partial_sum, "col")
            due_rows = (
                (due_rows.reshape(per_row * TB, width_k).astype(jnp.float32) - reached)
                .astype(jnp.bfloat16)
                .reshape(due_rows.shape)
            )
        gathered = lax.all_gather(due_rows, "row", axis=1, tiled=True).reshape(block_rows, width_k)
        columns = []
        for position in range(per_col):

            def compute(position=position):
                return jnp.dot(
                    dinv_rows[position, 0], gathered, preferred_element_type=jnp.float32
                ).astype(jnp.bfloat16)

            def retain(position=position):
                return solved[position, 0]

            columns.append(lax.cond(owners[position] == block, compute, retain))
        solved = jnp.stack(columns)[:, None]
    keep_trail = mask_trail.astype(jnp.bfloat16)[:, :, None, :, :, None]
    masked_trail = factor_trail * keep_trail
    share = rhs_trail.shape[1]
    moved = lax.all_to_all(masked_trail, "col", split_axis=0, concat_axis=4, tiled=True)
    reached = jnp.dot(
        moved.reshape(share * TB, -1),
        lax.all_gather(solved, "col", axis=1, tiled=True).reshape(-1, width_k),
        preferred_element_type=jnp.float32,
    )
    remaining = (rhs_trail.reshape(share * TB, width_k).astype(jnp.float32) - reached).astype(
        jnp.bfloat16
    )
    return (solved, remaining.reshape(rhs_trail.shape))


MESH = pl.DeviceIdType.MESH
F32 = jnp.float32
BF16 = jnp.bfloat16


def kernel(
    n_row, n_col,
    rhs_s, fac_s, mask_s, dinv, fac_t, mask_t, rhs_t,
    solved_o, rem_o,
    dinv_v, facs_v, fact_v, rhst_v, rhs1_v, ltri, due0, due1, dsh, part, rs0, solv, lt, acc, tpart, trs,
    local_sem, pair_send, pair_recv, z_send, z_recv, g_send, g_recv, f_send, f_recv, p_send, p_recv,
    s_send, s_recv, e_send, e_recv, t_send, t_recv,
):
    per_sb = dinv_v.shape[0] // NSB
    per_col = dinv_v.shape[0]
    sq_count, halves, sh, kr = due0.shape[0], due0.shape[2], due0.shape[3], due0.shape[4]
    sh2 = sh // 2
    tiles_t = fact_v.shape[0]
    share_t = tiles_t // n_col
    th = TB // 2
    cols = per_sb * TB
    n_chip = n_col // 2
    r, c = lax.axis_index("row"), lax.axis_index("col")
    chip, core = c // 2, c % 2
    other = 1 - core
    sib = chip * 2 + other
    sq, half = c // halves, c % halves
    rows_at = lambda d: lax.rem(r + d, n_row)
    cols_at = lambda d: lax.rem(c + d, n_col)

    barrier = pltpu.get_barrier_semaphore()
    for d in range(1, n_row):
        pl.semaphore_signal(barrier, inc=1, device_id=(rows_at(d), c), device_id_type=MESH)
    for d in range(1, n_col):
        pl.semaphore_signal(barrier, inc=1, device_id=(r, cols_at(d)), device_id_type=MESH)

    def kslice(k):
        return pl.ds(pl.multiple_of(k * kr, kr), kr)

    own_rows = pl.ds(pl.multiple_of(half * sh, sh), sh)
    local = [
        pltpu.make_async_copy(fac_s.at[1], facs_v, local_sem.at[0]),
        pltpu.make_async_copy(rhs_s.at[0, sq, own_rows, kslice(r)], due0.at[sq, r, half], local_sem.at[1]),
        pltpu.make_async_copy(fac_t, fact_v, local_sem.at[2]),
        pltpu.make_async_copy(dinv, dinv_v, local_sem.at[3]),
    ]
    for k in range(2):
        rows = pl.ds(pl.multiple_of(half * sh + k * sh2, sh2), sh2)
        local.append(pltpu.make_async_copy(rhs_s.at[1, sq, rows], rhs1_v.at[k], local_sem.at[4 + k]))
    local.append(pltpu.make_async_copy(rhs_t, rhst_v, local_sem.at[6]))
    for copy in local:
        copy.start()

    def sorter(count):
        shape = (count * TB, per_col * TB)
        a = lax.broadcasted_iota(jnp.int32, shape, 0)
        b = lax.broadcasted_iota(jnp.int32, shape, 1)
        return (b == (a % TB) * per_col + a // TB).astype(F32).astype(BF16)

    sort_all = sorter(per_col)
    local[0].wait()
    for q in range(sq_count):
        tiles = jnp.dot(sort_all[:cols], facs_v[q], preferred_element_type=F32)
        for p in range(per_sb):
            kept = (tiles[p * TB:(p + 1) * TB] * mask_s[1, q, p].astype(F32)).astype(BF16)
            for h in range(halves):
                for k in range(2):
                    at = (q * halves + h) * sh2
                    ltri[k, core, at:at + sh2, p * TB:(p + 1) * TB] = kept[h * sh + k * sh2:h * sh + (k + 1) * sh2]
    pl.semaphore_wait(barrier, n_row - 1 + n_col - 1)
    started = []

    def remote(src, dst, send, recv, device):
        copy = pltpu.make_async_remote_copy(
            src_ref=src, dst_ref=dst, send_sem=send, recv_sem=recv, device_id=device, device_id_type=MESH
        )
        started.append(copy)
        copy.start()
        return copy

    z0 = [
        remote(rhs_s.at[0, sq, own_rows, kslice(rows_at(d))], due0.at[sq, r, half],
               z_send.at[0, d - 1], z_recv.at[0, d - 1], (rows_at(d), c))
        for d in range(1, n_row)
    ]
    pair_l = remote(ltri.at[other, core], ltri.at[other, core], pair_send.at[0], pair_recv.at[0], (r, sib))

    def gather(due, s):
        own = due.at[sq, :, half]
        copies = [
            remote(own, own, g_send.at[s, e], g_recv.at[s, e], (r, lax.rem(chip + e, n_chip) * 2 + core))
            for e in range(1, n_chip)
        ]
        return [remote(own, own, g_send.at[s, 0], g_recv.at[s, 0], (r, sib))] + copies

    def gathered(due, s, copies):
        passed = []
        for e in range(1, n_chip):
            copies[e].wait_recv()
            came = lax.rem(chip + n_chip - e, n_chip) * 2 + core
            slot = due.at[came // halves, :, came % halves]
            passed.append(remote(slot, slot, f_send.at[s, e - 1], f_recv.at[s, e - 1], (r, sib)))
        copies[0].wait_recv()
        for copy in passed:
            copy.wait_recv()

    def solve(due, s):
        block = dinv_v[s * per_sb:(s + 1) * per_sb].reshape(cols, -1)
        fresh = jnp.dot(block, due[...].reshape(-1, kr), preferred_element_type=F32)
        solv[s, r, core] = fresh.astype(BF16)
        own = solv.at[s, r, core]
        near = remote(own, own, e_send.at[s, 0], e_recv.at[s, 0], (r, sib))
        return [near] + [
            remote(own, own, s_send.at[s, d - 1], s_recv.at[s, d - 1], (rows_at(d), c)) for d in range(1, n_row)
        ]

    def slice_ready(s, d, copies):
        copies[d].wait_recv()
        if d > 0:
            slot = solv.at[s, rows_at(n_row - d), core]
            remote(slot, slot, e_send.at[s, d], e_recv.at[s, d], (r, sib)).wait_recv()

    local[1].wait()
    for copy in z0:
        copy.wait_recv()
    g0 = gather(due0, 0)

    local[2].wait()

    def order(i, _):
        tiles = jnp.dot(sort_all, fact_v[i], preferred_element_type=F32)
        for p in range(per_col):
            kept = (tiles[p * TB:(p + 1) * TB] * mask_t[p, i].astype(F32)).astype(BF16)
            for k in range(2):
                lt[k, core, pl.ds(pl.multiple_of(i * th, th), th), p * TB:(p + 1) * TB] = kept[k * th:(k + 1) * th]
        return 0

    lax.fori_loop(0, tiles_t, order, 0)
    local[3].wait()
    gathered(due0, 0, g0)
    s0 = solve(due0, 0)
    pair_l.wait_recv()
    local[4].wait()
    local[5].wait()

    p_copies = []
    for d in range(n_row):
        at = rows_at(n_row - d)
        slice_ready(0, d, s0)
        update = jnp.dot(ltri[core, 0], solv[0, at, 0], preferred_element_type=F32)
        update += jnp.dot(ltri[core, 1], solv[0, at, 1], preferred_element_type=F32)
        part[at] = update.astype(BF16).reshape(n_col, sh2, kr)
        p_copies.append([
            remote(part.at[at, cols_at(e)], rs0.at[d, e - 1], p_send.at[d, e - 1], p_recv.at[d, e - 1], (r, cols_at(e)))
            for e in range(1, n_col)
        ])
    pair_t = remote(lt.at[other, core], lt.at[other, core], pair_send.at[1], pair_recv.at[1], (r, sib))

    def total(own, landed, copies):
        same, far = own.astype(F32), None
        for e in range(1, n_col):
            copies[e - 1].wait_recv()
            came = landed[e - 1].astype(F32)
            if e % 2 == 0:
                same += came
            else:
                far = came if far is None else far + came
        return same, far

    z1 = []
    for d in range(n_row):
        at = rows_at(n_row - d)
        for k, reached in zip((core, other), total(part[at, c], rs0.at[d], p_copies[d])):
            due = (rhs1_v[k, :, kslice(at)].astype(F32) - reached).astype(BF16)
            if d == 0:
                due1[sq, r, half, k] = due
            else:
                dsh[at, k] = due
        if d > 0:
            z1.append(remote(dsh.at[at], due1.at[sq, r, half], z_send.at[1, d - 1], z_recv.at[1, d - 1], (at, c)))
    for copy in z1:
        copy.wait_recv()
    g1 = gather(due1, 1)

    pair_t.wait_recv()
    for k in range(n_row):
        update = jnp.dot(lt[core, 0, :, :cols], solv[0, k, 0], preferred_element_type=F32)
        acc[k] = update + jnp.dot(lt[core, 1, :, :cols], solv[0, k, 1], preferred_element_type=F32)
    gathered(due1, 1, g1)
    s1 = solve(due1, 1)

    t_copies = []
    for d in range(n_row):
        at = rows_at(n_row - d)
        slice_ready(1, d, s1)
        update = acc[at] + jnp.dot(lt[core, 0, :, cols:], solv[1, at, 0], preferred_element_type=F32)
        update += jnp.dot(lt[core, 1, :, cols:], solv[1, at, 1], preferred_element_type=F32)
        tpart[at] = update.astype(BF16).reshape(n_col, -1, kr)
        t_copies.append([
            remote(tpart.at[at, cols_at(e)], trs.at[d, e - 1], t_send.at[d, e - 1], t_recv.at[d, e - 1], (r, cols_at(e)))
            for e in range(1, n_col)
        ])
    for s in range(NSB):
        for k in range(n_row):
            for_core = solv[s, k, core]
            solved_o[s * per_sb:(s + 1) * per_sb, :, k * kr:(k + 1) * kr] = for_core.reshape(per_sb, TB, kr)
    local[6].wait()
    for d in range(n_row):
        at = rows_at(n_row - d)
        for k, reached in zip((core, other), total(tpart[at, c], trs.at[d], t_copies[d])):
            for t in range(share_t):
                here = rhst_v[t, k, :, kslice(at)].astype(F32) - reached[t * th:(t + 1) * th]
                rem_o[t, k, :, kslice(at)] = here.astype(BF16)
    for copy in started:
        copy.wait_send()


def fast_body(n_row, n_col, rhs_super, factor_super, mask_super, dinv_rows, factor_trail, mask_trail, rhs_trail):
    width_k = rhs_super.shape[-1]
    sq_count = rhs_super.shape[1]
    per_col = dinv_rows.shape[0]
    tiles_t = factor_trail.shape[0]
    share_t = rhs_trail.shape[1]
    per_sb = per_col // NSB
    cols = per_sb * TB
    kr = width_k // n_row
    sh = sq_count * TB // n_col
    halves = TB // sh
    vmem = lambda *shape: pltpu.VMEM(shape, BF16)
    dma = lambda *shape: pltpu.SemaphoreType.DMA(shape)
    sh2, th, n_chip = sh // 2, TB // 2, n_col // 2
    anywhere = pl.BlockSpec(memory_space=pl.ANY)
    scalars = pl.BlockSpec(memory_space=pltpu.SMEM)
    whole = pl.BlockSpec(memory_space=pltpu.VMEM)
    solved, remaining = pl.pallas_call(
        functools.partial(kernel, n_row, n_col),
        out_shape=(
            jax.ShapeDtypeStruct((per_col, TB, width_k), BF16),
            jax.ShapeDtypeStruct((share_t, 2, th, width_k), BF16),
        ),
        in_specs=[anywhere, anywhere, scalars, anywhere, anywhere, scalars, anywhere],
        out_specs=(whole, whole),
        scratch_shapes=[
            vmem(per_col, TB, dinv_rows.shape[-1]),
            vmem(sq_count, TB * per_col, TB),
            vmem(tiles_t, TB * per_col, TB),
            vmem(share_t, 2, th, width_k),
            vmem(2, sh2, width_k),
            vmem(2, 2, n_col * sh2, cols),
            vmem(sq_count, n_row, halves, sh, kr),
            vmem(sq_count, n_row, halves, 2, sh2, kr),
            vmem(n_row, 2, sh2, kr),
            vmem(n_row, n_col, sh2, kr),
            vmem(n_row, n_col - 1, sh2, kr),
            vmem(NSB, n_row, 2, cols, kr),
            vmem(2, 2, tiles_t * th, per_col * TB),
            pltpu.VMEM((n_row, tiles_t * th, kr), F32),
            vmem(n_row, n_col, share_t * th, kr),
            vmem(n_row, n_col - 1, share_t * th, kr),
            dma(7),
            dma(2), dma(2),
            dma(NSB, n_row - 1), dma(NSB, n_row - 1),
            dma(NSB, n_chip), dma(NSB, n_chip),
            dma(NSB, n_chip - 1), dma(NSB, n_chip - 1),
            dma(n_row, n_col - 1), dma(n_row, n_col - 1),
            dma(NSB, n_row - 1), dma(NSB, n_row - 1),
            dma(NSB, n_row), dma(NSB, n_row),
            dma(n_row, n_col - 1), dma(n_row, n_col - 1),
        ],
        compiler_params=pltpu.CompilerParams(
            collective_id=0, has_side_effects=True, vmem_limit_bytes=60 * 1024 * 1024
        ),
    )(
        rhs_super.reshape(NSB, sq_count, TB, width_k),
        factor_super.reshape(NSB, sq_count, TB * per_col, TB),
        mask_super.reshape(NSB, sq_count, per_col),
        dinv_rows.reshape(per_col, TB, -1),
        factor_trail.reshape(tiles_t, TB * per_col, TB),
        mask_trail.reshape(tiles_t, per_col).T,
        rhs_trail.reshape(share_t, 2, th, width_k),
    )
    return solved[:, None], remaining.reshape(rhs_trail.shape)


def body_for(mesh):
    n_row, n_col = mesh.shape["row"], mesh.shape["col"]

    def body(rhs_super, factor_super, mask_super, dinv_rows, factor_trail, mask_trail, rhs_trail):
        args = (rhs_super, factor_super, mask_super, dinv_rows, factor_trail, mask_trail, rhs_trail)
        due_rows = rhs_super.shape[1] * TB
        fits = (
            ST % n_col == 0
            and due_rows % n_col == 0
            and TB % (due_rows // n_col) == 0
            and (due_rows // n_col) % 32 == 0
            and n_col % 2 == 0
            and rhs_super.shape[-1] % (n_row * 128) == 0
        )
        return fast_body(n_row, n_col, *args) if fits else plain_body(*args)

    return body


def solution(mesh):
    placed = (
        P(None, None, "row", None, None),
        P(None, None, "row", None, None, "col", None),
        P(None, None, "row", None, "col"),
        P(None, "col", None, None),
        P(None, "row", None, None, "col", None),
        P(None, "row", None, "col"),
        P("col", None, "row", None, None),
    )
    return jax.shard_map(
        body_for(mesh),
        mesh=mesh,
        in_specs=placed,
        out_specs=(P(None, "col", None, None), P("col", None, "row", None, None)),
        check_vma=False,
    )
```
